256 devices in a mesh: row: 32 (over z, x), col: 8 (over y, core).
Axes of the slice: x: 4, y: 4, z: 8, core: 2. Of those that a mesh axis runs over, the one named last changes fastest.
Arguments:
- activations: bfloat16 [2048, 16384], P('col', 'row'), may hold values from -6 to 6
- out_grads: bfloat16 [2048, 26624], P('row', 'col'), may hold values from -0.125 to 0.125
- weights: bfloat16 [16384, 26624], P('row', 'col'), may hold values from -0.119628906 to 0.119628906
- projector: bfloat16 [256, 16384], P(None, 'row')
- first_moment: float32 [256, 26624], P('row', 'col'), may hold values from -4 to 4
- second_moment: float32 [256, 26624], P('row', 'col'), may hold values from 1e-06 to 0.03
Outputs:
- new_weights: bfloat16 [16384, 26624], P('row', 'col')
- new_first: float32 [256, 26624], P('row', 'col')
- new_second: float32 [256, 26624], P('row', 'col')
The draws below stay inside these ranges and needn't reach their ends.
All inputs are finite; a program needn't handle non-finite values.
Results may differ from the reference program's by a relative error of at most 0.01005.
Values may be sent and summed in bfloat16 or wider, within the bound.
A program may use at most 64 MiB of HBM per device.

```python
import math
import jax
import jax.numpy as jnp
from jax import lax

D = 16384
FW = 26624
RANK = 256
TOKENS = 2048
STEP = 10
N_COL = 8


def draw_projector(key, part):
    key = jax.random.fold_in(key, 7)
    row_key, entry_key = jax.random.split(key)
    row_scales = jnp.exp(jax.random.uniform(row_key, (RANK, 1), jnp.float32, math.log(0.25), math.log(4.0)))
    entries = jnp.clip(jax.random.normal(entry_key, (RANK, D), jnp.float32), -4.0, 4.0)
    return (entries * row_scales / math.sqrt(D)).astype(jnp.bfloat16)


def level_of(stream_key, extent, shards, smallest, top_value):
    gain, own = 1.0, jax.random.fold_in(stream_key, 6)
    for axis_at, blocks in shards:
        heights = jnp.exp(jax.random.uniform(jax.random.fold_in(own, axis_at), (blocks,), jnp.float32, smallest / len(shards), top_value / len(shards)))
        gain = gain * jnp.repeat(heights, extent[axis_at] // blocks).reshape([-1 if axis == axis_at else 1 for axis in range(len(extent))])
    return gain


def scatter_about(key, dims, deviation, reach, cuts=(), kind=jnp.bfloat16):
    factor_of = level_of(key, dims, cuts, -0.22, 0.18) if cuts else 1.0
    result = jax.random.normal(key, dims, jnp.float32) * deviation * factor_of
    return jnp.minimum(jnp.maximum(result, -reach), reach).astype(kind)


def setup_inputs(seed: int = 0) -> dict:
    seeds = jax.random.split(jax.random.key(seed), 7)
    activations = scatter_about(seeds[0], (TOKENS, D), 1.0, 6.0, ((0, 8), (1, 32)))
    out_grads = scatter_about(seeds[1], (TOKENS, FW), TOKENS ** -0.5, 0.125, ((0, 32), (1, 8)))
    weights = scatter_about(seeds[2], (D, FW), 0.02, 0.119628906, ((0, 32), (1, 8)))
    projector = draw_projector(jax.random.fold_in(seeds[6], 71), 0)
    first_moment = scatter_about(seeds[4], (RANK, FW), 0.5, 4.0, ((0, 32), (1, 8)), jnp.float32)
    second_moment = jnp.clip(jnp.exp(math.log(0.03) - 10.3089526 * jax.random.uniform(seeds[5], (RANK, FW), jnp.float32) ** level_of(seeds[5], (RANK, FW), ((0, 32), (1, 8)), -0.2, 0.2)), 9.999999974752427e-07, 0.03)
    return {"activations": activations, "out_grads": out_grads, "weights": weights, "projector": projector, "first_moment": first_moment, "second_moment": second_moment}


def reference(activations, out_grads, weights, projector, first_moment, second_moment):
    width = FW // N_COL
    wide_projector = projector.astype(jnp.float32)
    firsts = []
    seconds = []
    updated = []
    for block in range(N_COL):
        start = block * width
        grads_blk = out_grads[:, start:start + width]
        grad_full = jnp.dot(activations.T, grads_blk, preferred_element_type=jnp.float32)
        grad = grad_full.astype(jnp.bfloat16)
        proj = jnp.dot(wide_projector, grad_full, precision=lax.Precision.HIGHEST)
        first = 0.9 * first_moment[:, start:start + width] + 0.1 * proj
        second = 0.999 * second_moment[:, start:start + width] + 0.001 * proj * proj
        normed = first / (1.0 - 0.9 ** STEP) / (jnp.sqrt(second / (1.0 - 0.999 ** STEP)) + 1e-08)
        scale = jnp.sqrt(lax.optimization_barrier(jnp.sum(normed * normed, axis=0))) / jnp.sqrt(lax.optimization_barrier(jnp.sum(proj * proj, axis=0)) + 1e-06)
        new_blk = weights[:, start:start + width].astype(jnp.float32) - 0.01 * scale[None, :] * grad.astype(jnp.float32)
        firsts.append(first)
        seconds.append(second)
        updated.append(new_blk.astype(jnp.bfloat16))
    return (jnp.concatenate(updated, axis=1), jnp.concatenate(firsts, axis=1), jnp.concatenate(seconds, axis=1))
```

```python
import jax
import jax.numpy as jnp
from jax import lax
from jax.experimental import pallas as pl
from jax.experimental.pallas import tpu as pltpu
from jax.sharding import PartitionSpec as P

STEP = 10
MESH = pl.DeviceIdType.MESH
BF = jnp.bfloat16
F32 = jnp.float32

NZ, NX, NY = 8, 4, 4
NCH = 13
LAG = 2
FIRST_C = 5 + LAG
TICKS = NCH + FIRST_C + 3


def kernel(
    act, og, w, pj, m1, m2, ow, o1, o2,
    avm, ogv, pv, wv, m1v, m2v, at, av1, g, gs, gr, go, ps, pr, po,
    s1s, s1r, s2s, s2r, qpart, qx, qs, qz, qsend,
    loc, r_p, r_b, r_z, r_m, r_g, r_pr, r_s1, r_s2, r_a, r_h, r_q, snd, outs,
):
    row, col = lax.axis_index("row"), lax.axis_index("col")
    z, x = row // 4, lax.rem(row, 4)
    y, core = col // 2, lax.rem(col, 2)
    pair_x = x + 1 - 2 * lax.rem(x, 2)
    mate_x = 3 - x
    cls = lax.rem((x + 1) // 2, 2)

    def at_z(d):
        return (lax.rem(z + d, NZ) * 4 + x, col)

    def at_x(d):
        return (z * 4 + lax.rem(x + d, NX), col)

    def at_y(d):
        return (row, lax.rem(y + d, NY) * 2 + core)

    def at_col(d):
        return (row, lax.rem(col + d, 8))

    up, down = at_z(1), at_z(NZ - 1)
    pair, mate = (z * 4 + pair_x, col), (z * 4 + mate_x, col)
    y_up, y_down = at_y(1), at_y(NY - 1)
    sibling = (row, y * 2 + 1 - core)

    def send(src, dst, ssem, rsem, target):
        pltpu.make_async_remote_copy(
            src_ref=src, dst_ref=dst, send_sem=ssem, recv_sem=rsem, device_id=target, device_id_type=MESH
        ).start()

    def wait(ref, sem):
        pltpu.make_async_copy(ref, ref, sem).wait()

    barrier = pltpu.get_barrier_semaphore()
    partners = [at_z(d) for d in range(1, NZ)] + [at_x(d) for d in range(1, NX)] + [at_col(d) for d in range(1, 8)]
    for partner in partners:
        pl.semaphore_signal(barrier, inc=1, device_id=partner, device_id_type=MESH)

    loads = [(act, avm), (og, ogv), (pj, pv), (w, wv), (m1, m1v), (m2, m2v)]
    for k, (src, dst) in enumerate(loads):
        pltpu.make_async_copy(src, dst, loc.at[k]).start()

    own_lanes = pl.ds(pl.multiple_of(col * 256, 256), 256)
    PAIR, OWN = 0, 528
    pltpu.make_async_copy(act, avm, loc.at[0]).wait()

    def turned(xx):
        parts = []
        for j in range(4):
            lo = lax.rem(xx, 2)
            hi = xx // 2
            lo = 1 - lo if j % 2 else lo
            hi = 1 - hi if j // 2 else hi
            parts.append(avm[pl.ds(pl.multiple_of((hi * 2 + lo) * 64, 64), 64), :])
        return jnp.concatenate(parts, axis=0).T

    av1[...] = turned(pair_x)
    at[pl.ds(OWN, 512), own_lanes] = turned(x)
    pltpu.make_async_copy(og, ogv, loc.at[1]).wait()
    pl.semaphore_wait(barrier, len(partners))

    def block(zz, start, size):
        return pl.ds(pl.multiple_of(zz * 256 + start, 32), size)

    def zrel(d):
        return lax.rem(z + d, NZ)

    def columns(which, c):
        return pl.ds(pl.multiple_of((which * NCH + c) * 128, 128), 128)

    S_Z, S_M, S_P, S_G, S_PR, S_S1, S_S2, S_AP, S_AO, S_H, S_QX, S_QZ, S_QC, S_QP = range(14)

    def p_stage(c):
        send(ogv.at[:, columns(1 - cls, c)], g.at[c, block(z, 64, 64)], snd.at[S_P], r_p.at[c], pair)

    def b1_stage(c):
        wait(g.at[c, block(z, 64, 64)], r_p.at[c])
        send(g.at[c, block(z, 64, 64)], g.at[c, block(z, 128, 64)], snd.at[S_M], r_b.at[c], mate)

    def b2_stage(c):
        wait(g.at[c, block(z, 128, 64)], r_b.at[c])
        part = g.at[c, block(z, 64, 128)]
        send(part, part, snd.at[S_Z], r_z.at[c, 0], up)
        send(part, part, snd.at[S_Z], r_z.at[c, 1], down)

    def to_mate(c, zz):
        send(g.at[c, block(zz, 0, 64)], g.at[c, block(zz, 192, 64)], snd.at[S_M], r_m.at[c], mate)

    def e0_stage(c):
        g[c, block(z, 0, 64), :] = ogv[:, columns(cls, c)]
        part = g.at[c, block(z, 0, 64)]
        send(part, part, snd.at[S_Z], r_z.at[c, 0], up)
        send(part, part, snd.at[S_Z], r_z.at[c, 1], down)
        to_mate(c, z)

    def z_stage(c, hop):
        lower, upper = zrel(NZ - hop), zrel(hop)
        if hop == 4:
            wait(g.at[c, block(lower, 0, 192)], r_z.at[c, 6])
            to_mate(c, lower)
            return
        a, b = (0, 192) if hop < 3 else (0, 96)
        wait(g.at[c, block(lower, 0, 192)], r_z.at[c, 2 * hop - 2])
        part = g.at[c, block(lower, a, b)]
        send(part, part, snd.at[S_Z], r_z.at[c, 2 * hop if hop < 3 else 6], up)
        a, b = (0, 192) if hop < 3 else (96, 96)
        wait(g.at[c, block(upper, 0, 192)], r_z.at[c, 2 * hop - 1])
        part = g.at[c, block(upper, a, b)]
        send(part, part, snd.at[S_Z], r_z.at[c, 2 * hop + 1 if hop < 3 else 6], down)
        to_mate(c, lower)
        to_mate(c, upper)

    def a_ref(panel, yy, start, size):
        lanes = pl.ds(pl.multiple_of((yy * 2 + core) * 256, 256), 256)
        return at.at[pl.ds((PAIR, OWN)[panel] + start, size), lanes]

    def a_send(panel, yy, start, size, sem, target):
        part = a_ref(panel, yy, start, size)
        send(part, part, snd.at[S_AP + panel], r_a.at[panel, sem], target)

    def a_start(panel, h):
        if panel == 0:
            wait(a_ref(0, y, 256 * h, 256), r_h.at[h])
        a_send(panel, y, 256 * h, 256, h, y_up)
        a_send(panel, y, 256 * h, 256, 2 + h, y_down)
        a_send(panel, y, 256 * h, 256, 6, sibling)

    y_lower, y_upper, y_far = lax.rem(y + 3, NY), lax.rem(y + 1, NY), lax.rem(y + 2, NY)

    def a_arrive(panel, h):
        wait(a_ref(panel, y_lower, 256 * h, 256), r_a.at[panel, h])
        if h == 0:
            a_send(panel, y_lower, 0, 256, 4, y_up)
        wait(a_ref(panel, y_upper, 256 * h, 256), r_a.at[panel, 2 + h])
        if h == 1:
            a_send(panel, y_upper, 256, 256, 5, y_down)
        a_send(panel, y_lower, 256 * h, 256, 6, sibling)
        a_send(panel, y_upper, 256 * h, 256, 6, sibling)

    def a_far(panel):
        wait(a_ref(panel, y_far, 0, 256), r_a.at[panel, 4])
        wait(a_ref(panel, y_far, 256, 256), r_a.at[panel, 5])
        a_send(panel, y_far, 0, 512, 6, sibling)

    def a_done(panel):
        wait(at.at[pl.ds((PAIR, OWN)[panel], 512), pl.ds(0, 1024)], r_a.at[panel, 6])

    def q_part():
        pltpu.make_async_copy(pj, pv, loc.at[2]).wait()
        q = lax.dot_general(pv[...], avm[...], (((1,), (1,)), ((), ())), preferred_element_type=F32)
        for xx in range(NX):
            for zz in range(NZ):
                start = 8 * (4 * zz + xx)
                qpart[xx, zz] = q[start : start + 8]
        for d in range(1, NX):
            send(qpart.at[lax.rem(x + d, NX)], qx.at[d - 1], snd.at[S_QX], r_q.at[0], at_x(d))

    def q_over_x():
        wait(qx, r_q.at[0])
        qs[...] = qpart[x] + qx[0] + qx[1] + qx[2]
        for d in range(1, NZ):
            send(qs.at[zrel(d)], qz.at[d - 1], snd.at[S_QZ], r_q.at[1], at_z(d))

    q_rows = at.at[pl.ds(OWN + 512, 16), own_lanes]

    def q_over_z():
        wait(qz, r_q.at[1])
        q = qs[z]
        for d in range(NZ - 1):
            q = q + qz[d]
        left, right = q[:, :128], q[:, 128:]
        odd = lax.rem(x, 2) == 1
        left = jnp.where(odd, pltpu.roll(left, 64, 1), left)
        right = jnp.where(odd, pltpu.roll(right, 64, 1), right)
        late = x >= 2
        q = jnp.concatenate([jnp.where(late, right, left), jnp.where(late, left, right)], axis=1)
        high = q.astype(BF).astype(F32)
        at[pl.ds(OWN + 512, 16), own_lanes] = jnp.concatenate([high, q - high], axis=0).astype(BF)
        for d in range(1, 8):
            send(q_rows, q_rows, snd.at[S_QC], r_q.at[2], at_col(d))

    def q_to_pair():
        wait(at.at[pl.ds(OWN + 512, 16), pl.ds(0, 1792)], r_q.at[2])
        for k in range(16):
            part = at[pl.ds(OWN + 512, 16), pl.ds(128 * k, 128)].astype(F32)
            qsend[:, pl.ds(128 * k, 128)] = pltpu.roll(part, 64, 1).astype(BF)
        send(qsend, at.at[pl.ds(PAIR + 512, 16), :], snd.at[S_QP], r_q.at[3], pair)

    def c_stage(c):
        wait(g.at[c, pl.ds(0, 512)], r_m.at[c])
        total = jnp.dot(at[pl.ds(PAIR, 528), :], g[c], preferred_element_type=F32)
        gs[c] = total[:512].astype(BF)
        ps[c] = total[512:520] + total[520:528]
        send(ps.at[c], pr.at[c], snd.at[S_PR], r_pr.at[c], pair)
        send(gs.at[c], gr.at[c], snd.at[S_G], r_g.at[c], pair)
        total = jnp.dot(at[pl.ds(OWN, 528), :], g[c], preferred_element_type=F32)
        go[c] = total[:512].astype(BF)
        po[c] = total[512:520] + total[520:528]

    def moments(proj, cols):
        first = 0.9 * m1v[:, cols] + 0.1 * proj
        second = 0.999 * m2v[:, cols] + 0.001 * proj * proj
        m1v[:, cols] = first
        m2v[:, cols] = second
        normed = first / (1.0 - 0.9**STEP) / (jnp.sqrt(second / (1.0 - 0.999**STEP)) + 1e-08)
        return jnp.sum(normed * normed, axis=0, keepdims=True), jnp.sum(proj * proj, axis=0, keepdims=True)

    def s1_stage(c):
        wait(pr.at[c], r_pr.at[c])
        n_own, p_own = moments(po[c], columns(cls, c))
        n_oth, p_oth = moments(pr[c], columns(1 - cls, c))
        first = cls == 0
        s1s[c, 0:1] = jnp.where(first, n_own, n_oth)
        s1s[c, 1:2] = jnp.where(first, p_own, p_oth)
        s1s[c, 2:3] = jnp.where(first, n_oth, n_own)
        s1s[c, 3:4] = jnp.where(first, p_oth, p_own)
        s1s[c, 4:8] = jnp.zeros((4, 128), F32)
        for d in range(1, NX):
            send(s1s.at[c], s1r.at[c, d - 1], snd.at[S_S1], r_s1.at[c], at_x(d))

    def s2_stage(c):
        wait(s1r.at[c], r_s1.at[c])
        s2s[c] = s1s[c] + s1r[c, 0] + s1r[c, 1] + s1r[c, 2]
        for d in range(1, NZ):
            send(s2s.at[c], s2r.at[c, d - 1], snd.at[S_S2], r_s2.at[c], at_z(d))

    def update(cols, grad, scale):
        wv[:, cols] = (wv[:, cols].astype(F32) - 0.01 * scale * grad.astype(F32)).astype(BF)
        pltpu.make_async_copy(wv.at[:, cols], ow.at[:, cols], outs.at[0]).start()

    def s3_stage(c):
        wait(s2r.at[c], r_s2.at[c])
        sums = s2s[c]
        for d in range(NZ - 1):
            sums = sums + s2r[c, d]
        scale_a = jnp.sqrt(sums[0:1]) / jnp.sqrt(sums[1:2] + 1e-06)
        scale_b = jnp.sqrt(sums[2:3]) / jnp.sqrt(sums[3:4] + 1e-06)
        first = cls == 0
        update(columns(cls, c), go[c], jnp.where(first, scale_a, scale_b))
        wait(gr.at[c], r_g.at[c])
        update(columns(1 - cls, c), gr[c], jnp.where(first, scale_b, scale_a))

    for c in range(2):
        p_stage(c)
    e0_stage(0)
    for h in range(2):
        send(
            av1.at[pl.ds(256 * h, 256)], at.at[pl.ds(PAIR + 256 * h, 256), own_lanes],
            snd.at[S_H], r_h.at[h], pair,
        )
    a_start(1, 0)
    q_part()
    b1_stage(0)

    def once(i, ticks, f):
        pl.when(i == ticks)(f)

    def stage(c, f):
        pl.when(jnp.logical_and(c >= 0, c < NCH))(lambda: f(c))

    @pl.loop(0, TICKS)
    def _(i):
        for hop in (4, 3, 2, 1):
            stage(i - hop, lambda c, hop=hop: z_stage(c, hop))
        stage(i, b2_stage)
        stage(i + 1, e0_stage)
        stage(i + 1, b1_stage)
        stage(i + 2, p_stage)

        @pl.when(i == 1)
        def _():
            a_start(0, 0)
            q_over_x()

        @pl.when(i == 2)
        def _():
            a_start(0, 1)
            a_start(1, 1)

        @pl.when(i == 3)
        def _():
            a_arrive(1, 0)
            q_over_z()

        @pl.when(i == 4)
        def _():
            a_arrive(0, 0)
            a_arrive(0, 1)
            q_to_pair()

        @pl.when(i == 5)
        def _():
            a_arrive(1, 1)
            a_far(0)

        @pl.when(i == 6)
        def _():
            a_far(1)
            pltpu.make_async_copy(m1, m1v, loc.at[4]).wait()
            pltpu.make_async_copy(m2, m2v, loc.at[5]).wait()
            pltpu.make_async_copy(w, wv, loc.at[3]).wait()

        @pl.when(i == FIRST_C)
        def _():
            a_done(0)
            a_done(1)
            wait(qsend, r_q.at[3])

        stage(i - FIRST_C, c_stage)
        stage(i - FIRST_C - 3, s3_stage)
        stage(i - FIRST_C - 2, s2_stage)
        stage(i - FIRST_C - 1, s1_stage)

        @pl.when(i == FIRST_C + NCH)
        def _():
            pltpu.make_async_copy(m1v, o1, outs.at[1]).start()
            pltpu.make_async_copy(m2v, o2, outs.at[2]).start()

    wait(g.at[:, pl.ds(0, 1344)], snd.at[S_Z])
    wait(g.at[:, pl.ds(0, 576)], snd.at[S_M])
    wait(g.at[:, pl.ds(0, 64)], snd.at[S_P])
    wait(gs, snd.at[S_G])
    wait(ps, snd.at[S_PR])
    wait(s1r, snd.at[S_S1])
    wait(s2r, snd.at[S_S2])
    wait(at.at[pl.ds(0, 512), pl.ds(0, 1792)], snd.at[S_AP])
    wait(at.at[pl.ds(0, 512), pl.ds(0, 1792)], snd.at[S_AO])
    wait(av1, snd.at[S_H])
    wait(qx, snd.at[S_QX])
    wait(qz, snd.at[S_QZ])
    wait(at.at[pl.ds(0, 16), pl.ds(0, 1792)], snd.at[S_QC])
    wait(qsend, snd.at[S_QP])
    wait(m1v, outs.at[1])
    wait(m2v, outs.at[2])
    wait(wv, outs.at[0])


def shards(activations, out_grads, weights, projector, first_moment, second_moment):
    vm, dma = pltpu.VMEM, pltpu.SemaphoreType.DMA
    return pl.pallas_call(
        kernel,
        out_shape=(
            jax.ShapeDtypeStruct((512, 3328), BF),
            jax.ShapeDtypeStruct((8, 3328), F32),
            jax.ShapeDtypeStruct((8, 3328), F32),
        ),
        in_specs=[pl.BlockSpec(memory_space=pl.ANY)] * 6,
        out_specs=(pl.BlockSpec(memory_space=pl.ANY),) * 3,
        scratch_shapes=[
            vm((256, 512), BF),
            vm((64, 3328), BF),
            vm((256, 512), BF),
            vm((512, 3328), BF),
            vm((8, 3328), F32),
            vm((8, 3328), F32),
            vm((1056, 2048), BF),
            vm((512, 256), BF),
            vm((NCH, 2048, 128), BF),
            vm((NCH, 512, 128), BF),
            vm((NCH, 512, 128), BF),
            vm((NCH, 512, 128), BF),
            vm((NCH, 8, 128), F32),
            vm((NCH, 8, 128), F32),
            vm((NCH, 8, 128), F32),
            vm((NCH, 8, 128), F32),
            vm((NCH, 3, 8, 128), F32),
            vm((NCH, 8, 128), F32),
            vm((NCH, 7, 8, 128), F32),
            vm((4, 8, 8, 256), F32),
            vm((3, 8, 8, 256), F32),
            vm((8, 8, 256), F32),
            vm((7, 8, 256), F32),
            vm((16, 2048), BF),
            dma((6,)),
            dma((NCH,)),
            dma((NCH,)),
            dma((NCH, 7)),
            dma((NCH,)),
            dma((NCH,)),
            dma((NCH,)),
            dma((NCH,)),
            dma((NCH,)),
            dma((2, 7)),
            dma((2,)),
            dma((4,)),
            dma((14,)),
            dma((3,)),
        ],
        compiler_params=pltpu.CompilerParams(
            collective_id=0, has_side_effects=True, vmem_limit_bytes=48 * 1024 * 1024
        ),
    )(activations, out_grads, weights, projector, first_moment, second_moment)


def solution(mesh):
    return jax.shard_map(
        shards,
        mesh=mesh,
        in_specs=(
            P("col", "row"),
            P("row", "col"),
            P("row", "col"),
            P(None, "row"),
            P("row", "col"),
            P("row", "col"),
        ),
        out_specs=(P("row", "col"), P("row", "col"), P("row", "col")),
        check_vma=False,
    )
```

```python
import jax
import jax.numpy as jnp
from jax import lax
from jax.experimental import pallas as pl
from jax.experimental.pallas import tpu as pltpu
from jax.sharding import PartitionSpec as P

STEP = 10
MESH = pl.DeviceIdType.MESH
BF = jnp.bfloat16
F32 = jnp.float32

NZ, NX, NY = 8, 4, 4
NT = 26
NCH = 7
NU = 4

ORDER = [
    ("a_over_x", 3, 1), ("a_over_x", 1, 0), ("q_part",), ("a_start", 0, 0), ("a_start", 0, 1), ("x_send", 2),
    ("x_send", 1), ("a_relay", 1), ("a_relay", 3), ("z_hop", 0, 2), ("x_send", 3), ("a_start", 3, 0),
    ("a_over_x", 3, 0), ("z_hop", 0, 1), ("a_start", 2, 1), ("z_hop", 1, 2), ("x_send", 0), ("a_start", 2, 0),
    ("a_over_x", 1, 1), ("a_start", 1, 0), ("z_hop", 1, 1), ("z_hop", 2, 2), ("a_arrive", 2, 0), ("a_arrive", 2, 1),
    ("a_start", 3, 1), ("a_start", 1, 1), ("z_hop", 2, 1), ("z_hop", 3, 2), ("q_over_z",), ("a_arrive", 3, 0),
    ("m_send",), ("z_hop", 0, 0), ("a_far", 2), ("a_arrive", 1, 0), ("z_hop", 3, 1), ("z_hop", 0, 3),
    ("a_arrive", 3, 1), ("a_done", 2), ("z_hop", 4, 2), ("grad", 2, 2), ("a_arrive", 0, 0), ("a_arrive", 1, 1),
    ("q_over_x",), ("z_hop", 1, 0), ("z_hop", 4, 1), ("a_far", 3), ("grad", 2, 1), ("z_hop", 1, 3), ("a_done", 3),
    ("z_hop", 2, 0), ("a_far", 1), ("grad", 3, 1), ("a_done", 1), ("grad", 1, 1), ("grad", 1, 2), ("a_arrive", 0, 1),
    ("z_hop", 3, 0), ("z_hop", 2, 3), ("grad", 3, 2), ("m_done",), ("q_done",), ("sums", 1), ("z_hop", 4, 0),
    ("grad", 1, 0), ("z_hop", 3, 3), ("grad", 3, 0), ("sums", 0), ("sums", 2), ("z_hop", 4, 3), ("sums", 3),
    ("a_far", 0), ("scale", 1), ("grad", 3, 3), ("grad", 1, 3), ("scale", 2), ("a_done", 0), ("grad", 0, 2),
    ("scale", 0), ("grad", 2, 0), ("update", 3, 1), ("scale", 3), ("grad", 0, 3), ("grad", 2, 3), ("update", 0, 2),
    ("new_moments",), ("grad", 0, 0), ("update", 1, 2), ("update", 2, 2), ("update", 2, 1), ("update", 1, 1),
    ("update", 3, 2), ("grad", 0, 1), ("update", 1, 3), ("update", 0, 1), ("update", 3, 0), ("update", 2, 0),
    ("update", 1, 0), ("update", 0, 3), ("update", 3, 3), ("update", 0, 0), ("update", 2, 3),
]


def kernel(
    act, og, w, pj, m1, m2, ow, o1, o2,
    avm, ogv, pv, wv, m1v, m2v, at, qa, g, gs, gx, prv, pst, mw, s2s, s2r, scs, scr, qpart, qx, qs, qz,
    loc, r_x, r_z, r_g, r_pr, r_s2, r_sc, r_a, r_ax, r_m, r_q,
    snd_x, snd_z, snd_g, snd_pr, snd_s2, snd_sc, snd_a, snd_ax, snd_m, snd_q, outs,
):
    row, col = lax.axis_index("row"), lax.axis_index("col")
    z, x = row // 4, lax.rem(row, 4)
    y, core = col // 2, lax.rem(col, 2)

    def at_z(d):
        return (lax.rem(z + d, NZ) * 4 + x, col)

    def at_x(d):
        return (z * 4 + lax.rem(x + d, NX), col)

    def at_y(d):
        return (row, lax.rem(y + d, NY) * 2 + core)

    def at_col(d):
        return (row, lax.rem(col + d, 8))

    up, down = at_z(1), at_z(NZ - 1)
    y_up, y_down = at_y(1), at_y(NY - 1)
    sibling = (row, y * 2 + 1 - core)

    def tile_start(xx):
        late = jnp.maximum(xx - 2, 0)
        return jnp.where(core == 0, 7 * xx - late, 6 * xx + late)

    def tile_count(xx):
        return jnp.where((xx < 2) == (core == 0), 7, 6)

    def window_start(xx):
        return jnp.minimum(tile_start(xx), NT - NCH)

    def x_of(d):
        return lax.rem(x + d, NX)

    def zrel(d):
        return lax.rem(z + d, NZ)

    start, count = tile_start(x), tile_count(x)

    def send(src, dst, ssem, rsem, target):
        pltpu.make_async_remote_copy(
            src_ref=src, dst_ref=dst, send_sem=ssem, recv_sem=rsem, device_id=target, device_id_type=MESH
        ).start()

    def wait(ref, sem):
        pltpu.make_async_copy(ref, ref, sem).wait()

    def tile(t, n=1):
        return pl.ds(pl.multiple_of(t * 128, 128), n * 128)

    def zblock(zz, begin=0, size=256):
        return pl.ds(pl.multiple_of(zz * 256 + begin, 64), size)

    barrier = pltpu.get_barrier_semaphore()
    partners = [at_z(d) for d in range(1, NZ)] + [at_x(d) for d in range(1, NX)] + [at_col(d) for d in range(1, 8)]
    for partner in partners:
        pl.semaphore_signal(barrier, inc=1, device_id=partner, device_id_type=MESH)

    loads = [(og, ogv), (act, avm), (pj, pv), (m1, m1v), (m2, m2v), (w, wv)]
    for k, (src, dst) in enumerate(loads):
        pltpu.make_async_copy(src, dst, loc.at[k]).start()

    def loaded(k):
        pltpu.make_async_copy(*loads[k], loc.at[k]).wait()

    own_lanes = pl.ds(pl.multiple_of(col * 256, 256), 256)

    def panel_rows(xx, begin=0, size=512):
        return pl.ds(pl.multiple_of(xx * 512 + begin, 256), size)

    def first_tile(u):
        return max(2 * u - 1, 0)

    def with_width(u, tiles, f):
        if u < NU - 1:
            f(1 if u == 0 else 2)
        else:
            pl.when(tiles == NCH)(lambda: f(2))
            pl.when(tiles == NCH - 1)(lambda: f(1))

    def low(n):
        return pl.ds(0, 128 * n)

    loaded(1)
    at[panel_rows(x), own_lanes] = avm[...].T
    loaded(0)
    g_rows = zblock(z, 64 * x, 64)
    for u in range(NU):

        def keep(n, u=u):
            g[u, g_rows, low(n)] = ogv[:, tile(start + first_tile(u), n)]
            if n == 1:
                g[u, :, pl.ds(128, 128)] = jnp.zeros((2048, 128), BF)

        with_width(u, count, keep)
    mw[:, :, :, pl.ds(NCH * 128, 128)] = jnp.zeros((4, 2, 8, 128), F32)
    pl.semaphore_wait(barrier, len(partners))

    def x_send(u):
        for d in (2, 1, 3):
            xx = x_of(d)

            def go(n, d=d, xx=xx):
                mine = ogv.at[:, tile(tile_start(xx) + first_tile(u), n)]
                send(mine, g.at[u, g_rows, low(n)], snd_x.at[d - 1, u], r_x.at[u], at_x(d))

            with_width(u, tile_count(xx), go)

    def z_hop(hop, u):
        lower, upper = zrel(NZ - hop), zrel(hop)

        def go(n):
            def move(zz, a, b, sem, target):
                part = g.at[u, zblock(zz, a, b), low(n)]
                send(part, part, snd_z.at[u], r_z.at[u, sem], target)

            def arrive(zz, sem):
                wait(g.at[u, zblock(zz), low(n)], r_z.at[u, sem])

            if hop == 0:
                wait(g.at[u, pl.ds(0, 192), low(n)], r_x.at[u])
                move(z, 0, 256, 0, up)
                move(z, 0, 256, 1, down)
            elif hop == 4:
                arrive(lower, 6)
            else:
                last = hop == 3
                arrive(lower, 2 * hop - 2)
                move(lower, 0, 128 if last else 256, 6 if last else 2 * hop, up)
                arrive(upper, 2 * hop - 1)
                move(upper, 128 if last else 0, 128 if last else 256, 6 if last else 2 * hop + 1, down)

        with_width(u, count, go)

    def a_ref(d, yy, begin, size):
        lanes = pl.ds(pl.multiple_of((yy * 2 + core) * 256, 256), 256)
        return at.at[panel_rows(x_of(d), begin, size), lanes]

    def a_send(d, yy, begin, size, sem, target):
        part = a_ref(d, yy, begin, size)
        send(part, part, snd_a.at[d], r_a.at[d, sem], target)

    def a_over_x(d, h):
        part = at.at[panel_rows(x, 256 * h, 256), own_lanes]
        send(part, part, snd_ax, r_ax.at[NX - d, h], at_x(d))

    over_x_seen = set()

    def over_x(d, h):
        if (d, h) not in over_x_seen:
            over_x_seen.add((d, h))
            wait(a_ref(d, y, 256 * h, 256), r_ax.at[d, h])

    def a_relay(d):
        h = 0 if d == 3 else 1
        over_x(d, h)
        part = a_ref(d, y, 256 * h, 256)
        send(part, part, snd_ax, r_ax.at[2, h], at_x(NX - d))

    def a_start(d, h):
        if d:
            over_x(d, h)
        a_send(d, y, 256 * h, 256, h, y_up)
        a_send(d, y, 256 * h, 256, 2 + h, y_down)
        a_send(d, y, 256 * h, 256, 6, sibling)

    y_lower, y_upper, y_far = lax.rem(y + 3, NY), lax.rem(y + 1, NY), lax.rem(y + 2, NY)

    def a_arrive(d, h):
        wait(a_ref(d, y_lower, 256 * h, 256), r_a.at[d, h])
        if h == 0:
            a_send(d, y_lower, 0, 256, 4, y_up)
        wait(a_ref(d, y_upper, 256 * h, 256), r_a.at[d, 2 + h])
        if h == 1:
            a_send(d, y_upper, 256, 256, 5, y_down)
        a_send(d, y_lower, 256 * h, 256, 6, sibling)
        a_send(d, y_upper, 256 * h, 256, 6, sibling)

    def a_far(d):
        wait(a_ref(d, y_far, 0, 256), r_a.at[d, 4])
        wait(a_ref(d, y_far, 256, 256), r_a.at[d, 5])
        a_send(d, y_far, 0, 512, 6, sibling)

    def a_done(d):
        wait(at.at[pl.ds(0, 512), pl.ds(0, 1024)], r_a.at[d, 6])

    def q_part():
        loaded(2)
        q = lax.dot_general(pv[...], avm[...], (((1,), (1,)), ((), ())), preferred_element_type=F32)
        for zz in range(NZ):
            qpart[zz] = q[32 * zz : 32 * zz + 32]
        for d in range(1, NZ):
            send(qpart.at[zrel(d)], qz.at[d - 1], snd_q.at[0], r_q.at[0], at_z(d))

    def q_over_z():
        wait(qz, r_q.at[0])
        q = qpart[z]
        for d in range(NZ - 1):
            q = q + qz[d]
        qs[...] = q
        for d in (2, 1, 3):
            send(qs, qx.at[d - 1], snd_q.at[1], r_q.at[1], at_x(d))

    def q_over_x():
        wait(qx, r_q.at[1])
        q = qs[...] + qx[0] + qx[1] + qx[2]
        high = q.astype(BF).astype(F32)
        rest = q - high
        parts = []
        for xx in range(NX):
            parts += [high[8 * xx : 8 * xx + 8], rest[8 * xx : 8 * xx + 8]]
        qa[:, own_lanes] = jnp.concatenate(parts, axis=0).astype(BF)
        part = qa.at[:, own_lanes]
        for d in range(1, 8):
            send(part, part, snd_q.at[2], r_q.at[2], at_col(d))

    def q_done():
        wait(qa.at[:, pl.ds(0, 1792)], r_q.at[2])

    def m_send():
        loaded(3)
        loaded(4)
        own = tile(window_start(x), NCH)
        mw[x, 0, :, low(NCH)] = m1v[:, own]
        mw[x, 1, :, low(NCH)] = m2v[:, own]
        for d in range(1, NX):
            cols = tile(window_start(x_of(d)), NCH)
            send(m1v.at[:, cols], mw.at[x, 0, :, low(NCH)], snd_m, r_m, at_x(d))
            send(m2v.at[:, cols], mw.at[x, 1, :, low(NCH)], snd_m, r_m, at_x(d))

    def m_done():
        wait(mw.at[pl.ds(0, 3), :, :, low(NCH)], r_m)

    def grad(d, u):
        total = jnp.dot(at[panel_rows(x_of(d)), :], g[u], preferred_element_type=F32).astype(BF)
        if d:
            gs[d - 1, u] = total

        def go(n):
            cols = tile(start + first_tile(u), n)
            if d:
                send(gs.at[d - 1, u, :, low(n)], gx.at[:, cols], snd_g.at[u], r_g.at[NX - d - 1, u], at_x(d))
            else:
                gx[:, cols] = total[:, : 128 * n]

        with_width(u, count, go)

    def moments(first_moment, second_moment, proj):
        first = 0.9 * first_moment + 0.1 * proj
        second = 0.999 * second_moment + 0.001 * proj * proj
        return first, second

    def sums(u):
        total = jnp.dot(qa[...], g[u], preferred_element_type=F32)
        lanes = tile(start - window_start(x) + first_tile(u), 2)
        normed_sq = jnp.zeros((8, 256), F32)
        proj_sq = jnp.zeros((8, 256), F32)
        wide = 1 if u == 0 else 2
        for xx in range(NX):
            proj = total[16 * xx : 16 * xx + 8] + total[16 * xx + 8 : 16 * xx + 16]
            pst[xx, :, tile(first_tile(u), wide)] = proj[:, : 128 * wide]
            first, second = moments(mw[xx, 0, :, lanes], mw[xx, 1, :, lanes], proj)
            normed = first / (1.0 - 0.9**STEP) / (jnp.sqrt(second / (1.0 - 0.999**STEP)) + 1e-08)
            normed_sq = normed_sq + normed * normed
            proj_sq = proj_sq + proj * proj
        normed_sq = jnp.sum(normed_sq, axis=0, keepdims=True)
        proj_sq = jnp.sum(proj_sq, axis=0, keepdims=True)
        s2s[u, 0:1] = normed_sq[:, :128]
        s2s[u, 1:2] = proj_sq[:, :128]
        s2s[u, 2:3] = normed_sq[:, 128:]
        s2s[u, 3:4] = proj_sq[:, 128:]
        s2s[u, 4:8] = jnp.zeros((4, 128), F32)
        for d in range(1, NZ):
            send(s2s.at[u], s2r.at[u, d - 1], snd_s2.at[u], r_s2.at[u], at_z(d))
        if u == NU - 1:
            for tiles in (NCH - 1, NCH):

                @pl.when(count == tiles)
                def _(tiles=tiles):
                    cols = tile(start, tiles)
                    prv[:, cols] = pst[x, :, low(tiles)]
                    for d in (2, 1, 3):
                        send(pst.at[x_of(d), :, low(tiles)], prv.at[:, cols], snd_pr, r_pr.at[NX - d - 1], at_x(d))

    def scale(u):
        wait(s2r.at[u], r_s2.at[u])
        total = s2s[u]
        for d in range(NZ - 1):
            total = total + s2r[u, d]
        left = jnp.sqrt(total[0:1]) / jnp.sqrt(total[1:2] + 1e-06)
        right = jnp.sqrt(total[2:3]) / jnp.sqrt(total[3:4] + 1e-06)
        scs[u] = jnp.broadcast_to(jnp.concatenate([left, right], axis=1), (8, 256))

        def go(n):
            cols = tile(start + first_tile(u), n)
            scr[:, cols] = scs[u, :, low(n)]
            for d in (2, 1, 3):
                send(scs.at[u, :, low(n)], scr.at[:, cols], snd_sc.at[u], r_sc.at[NX - d - 1, u], at_x(d))

        with_width(u, count, go)

    weights_seen = []

    def update(d, u):
        back = (NX - d) % NX
        xx = x_of(back)
        if not weights_seen:
            weights_seen.append(True)
            loaded(5)

        def go(n):
            cols = tile(tile_start(xx) + first_tile(u), n)
            if d:
                wait(scr.at[:, cols], r_sc.at[back - 1, u])
                wait(gx.at[:, cols], r_g.at[back - 1, u])
            step = 0.01 * scr[0:1, cols]
            wv[:, cols] = (wv[:, cols].astype(F32) - step * gx[:, cols].astype(F32)).astype(BF)
            pltpu.make_async_copy(wv.at[:, cols], ow.at[:, cols], outs.at[0]).start()

        with_width(u, tile_count(xx), go)

    def new_moments():
        for d in range(1, NX):
            xx = x_of(d)
            for tiles in (NCH - 1, NCH):

                @pl.when(tile_count(xx) == tiles)
                def _(tiles=tiles):
                    wait(prv.at[:, tile(tile_start(xx), tiles)], r_pr.at[d - 1])

        wait(mw.at[pl.ds(0, 3), :, :, low(NCH)], snd_m)
        m1v[...], m2v[...] = moments(m1v[...], m2v[...], prv[...])
        pltpu.make_async_copy(m1v, o1, outs.at[1]).start()
        pltpu.make_async_copy(m2v, o2, outs.at[2]).start()

    steps = dict(
        x_send=x_send, z_hop=z_hop, a_over_x=a_over_x, a_relay=a_relay, a_start=a_start, a_arrive=a_arrive,
        a_far=a_far, a_done=a_done, q_part=q_part, q_over_z=q_over_z, q_over_x=q_over_x, q_done=q_done,
        m_send=m_send, m_done=m_done, grad=grad, sums=sums, scale=scale, update=update, new_moments=new_moments,
    )
    for name, *numbers in ORDER:
        steps[name](*numbers)

    for u in range(NU):

        def drain(n, u=u):
            wait(g.at[u, pl.ds(0, 1792), low(n)], snd_z.at[u])
            wait(gs.at[:, u, :, low(n)], snd_g.at[u])
            wait(scr.at[:, low(3 * n)], snd_sc.at[u])

        with_width(u, count, drain)
        wait(s2r.at[u], snd_s2.at[u])
        for d in range(1, NX):
            with_width(u, tile_count(x_of(d)), lambda n, u=u, d=d: wait(ogv.at[:, low(n)], snd_x.at[d - 1, u]))
    for tiles in (NCH - 1, NCH):
        pl.when(count == tiles)(lambda tiles=tiles: wait(pst.at[pl.ds(0, 3), :, low(tiles)], snd_pr))
    for d in range(NX):
        wait(at.at[pl.ds(0, 512), pl.ds(0, 1792)], snd_a.at[d])
    wait(at.at[pl.ds(0, 512), pl.ds(0, 768)], snd_ax)
    wait(qz, snd_q.at[0])
    wait(qx, snd_q.at[1])
    wait(qa.at[:, pl.ds(0, 1792)], snd_q.at[2])
    wait(m1v, outs.at[1])
    wait(m2v, outs.at[2])
    wait(wv, outs.at[0])


def shards(activations, out_grads, weights, projector, first_moment, second_moment):
    vm, dma = pltpu.VMEM, pltpu.SemaphoreType.DMA
    operands = (activations, out_grads, weights, projector, first_moment, second_moment)
    operands = [pltpu.with_memory_space_constraint(operand, pltpu.HBM) for operand in operands]
    return pl.pallas_call(
        kernel,
        out_shape=(
            jax.ShapeDtypeStruct((512, 3328), BF),
            jax.ShapeDtypeStruct((8, 3328), F32),
            jax.ShapeDtypeStruct((8, 3328), F32),
        ),
        in_specs=[pl.BlockSpec(memory_space=pl.ANY)] * 6,
        out_specs=(pl.BlockSpec(memory_space=pl.ANY),) * 3,
        scratch_shapes=[
            vm((256, 512), BF),
            vm((64, 3328), BF),
            vm((256, 512), BF),
            vm((512, 3328), BF),
            vm((8, 3328), F32),
            vm((8, 3328), F32),
            vm((2048, 2048), BF),
            vm((64, 2048), BF),
            vm((NU, 2048, 256), BF),
            vm((3, NU, 512, 256), BF),
            vm((512, 3328), BF),
            vm((8, 3328), F32),
            vm((4, 8, 1024), F32),
            vm((4, 2, 8, 1024), F32),
            vm((NU, 8, 128), F32),
            vm((NU, 7, 8, 128), F32),
            vm((NU, 8, 256), F32),
            vm((8, 3328), F32),
            vm((8, 32, 256), F32),
            vm((3, 32, 256), F32),
            vm((32, 256), F32),
            vm((7, 32, 256), F32),
            dma((6,)),
            dma((NU,)),
            dma((NU, 7)),
            dma((3, NU)),
            dma((3,)),
            dma((NU,)),
            dma((3, NU)),
            dma((NX, 7)),
            dma((NX, 2)),
            dma,
            dma((3,)),
            dma((3, NU)),
            dma((NU,)),
            dma((NU,)),
            dma,
            dma((NU,)),
            dma((NU,)),
            dma((NX,)),
            dma,
            dma,
            dma((3,)),
            dma((3,)),
        ],
        compiler_params=pltpu.CompilerParams(
            collective_id=0, has_side_effects=True, vmem_limit_bytes=48 * 1024 * 1024
        ),
    )(*operands)


def solution(mesh):
    return jax.shard_map(
        shards,
        mesh=mesh,
        in_specs=(
            P("col", "row"),
            P("row", "col"),
            P("row", "col"),
            P(None, "row"),
            P("row", "col"),
            P("row", "col"),
        ),
        out_specs=(P("row", "col"), P("row", "col"), P("row", "col")),
        check_vma=False,
    )
```

```python
import jax
import jax.numpy as jnp
from jax import lax
from jax.experimental import pallas as pl
from jax.experimental.pallas import tpu as pltpu
from jax.sharding import PartitionSpec as P

STEP = 10
MESH = pl.DeviceIdType.MESH
BF = jnp.bfloat16
F32 = jnp.float32

NZ, NX, NY = 8, 4, 4
NT = 26
NCH = 7
NU = 4

ORDER = [
    ("a_over_x", 3, 1), ("q_part",), ("x_send", 2), ("a_over_x", 1, 0), ("x_send", 1), ("a_start", 1, 1),
    ("a_over_x", 3, 0), ("z_hop", 0, 2), ("x_send", 0), ("a_start", 3, 0), ("a_over_x", 1, 1), ("z_hop", 0, 1),
    ("a_relay", 3), ("a_start", 1, 0), ("z_hop", 1, 2), ("a_start", 3, 1), ("z_hop", 1, 1), ("a_relay", 1),
    ("a_arrive", 3, 0), ("q_over_z",), ("a_arrive", 1, 1), ("a_arrive", 1, 0), ("z_hop", 2, 2), ("x_send", 3),
    ("a_arrive", 3, 1), ("a_start", 2, 0), ("z_hop", 2, 1), ("z_hop", 3, 2), ("m_send",), ("z_hop", 0, 0),
    ("a_far", 1), ("a_start", 2, 1), ("a_far", 3), ("z_hop", 3, 1), ("z_hop", 0, 3), ("a_done", 3), ("q_over_x",),
    ("a_done", 1), ("z_hop", 4, 2), ("grad", 1, 2), ("grad", 3, 2), ("a_arrive", 2, 0), ("z_hop", 1, 0),
    ("a_arrive", 2, 1), ("a_start", 0, 0), ("z_hop", 4, 1), ("m_done",), ("grad", 3, 1), ("z_hop", 1, 3),
    ("grad", 1, 1), ("q_done",), ("z_hop", 2, 0), ("a_start", 0, 1), ("sums", 1), ("a_far", 2), ("sums", 2),
    ("z_hop", 2, 3), ("a_done", 2), ("grad", 2, 2), ("z_hop", 3, 0), ("a_arrive", 0, 1), ("z_hop", 3, 3),
    ("z_hop", 4, 0), ("scale", 2), ("grad", 2, 0), ("scale", 1), ("sums", 0), ("a_arrive", 0, 0), ("z_hop", 4, 3),
    ("sums", 3), ("grad", 2, 3), ("grad", 3, 3), ("grad", 1, 3), ("update", 1, 2), ("a_far", 0), ("scale", 0),
    ("grad", 1, 0), ("update", 3, 1), ("a_done", 0), ("scale", 3), ("grad", 0, 1), ("proj_out",), ("grad", 0, 2),
    ("grad", 2, 1), ("grad", 0, 0), ("grad", 0, 3), ("update", 0, 2), ("grad", 3, 0), ("update", 1, 3),
    ("update", 1, 0), ("update", 2, 3), ("update", 0, 3), ("update", 1, 1), ("update", 3, 3), ("update", 3, 2),
    ("update", 0, 0), ("update", 0, 1), ("update", 2, 2), ("update", 2, 0), ("update", 2, 1), ("update", 3, 0),
]


def moments(first_moment, second_moment, proj):
    first = 0.9 * first_moment + 0.1 * proj
    second = 0.999 * second_moment + 0.001 * proj * proj
    return first, second


def kernel(
    act, og, w, pj, m1, m2, ow, o1,
    avm, ogv, pv, wv, m1v, m2v, at, qa, g, gs, gx, prv, pst, mw, s2s, s2r, scs, scr, qpart, qx, qs, qz,
    loc, r_x, r_z, r_g, r_pr, r_s2, r_sc, r_a, r_ax, r_m, r_q,
    snd_x, snd_z, snd_g, snd_pr, snd_s2, snd_sc, snd_a, snd_ax, snd_m, snd_q, outs,
):
    row, col = lax.axis_index("row"), lax.axis_index("col")
    z, x = row // 4, lax.rem(row, 4)
    y, core = col // 2, lax.rem(col, 2)

    def at_z(d):
        return (lax.rem(z + d, NZ) * 4 + x, col)

    def at_x(d):
        return (z * 4 + lax.rem(x + d, NX), col)

    def at_y(d):
        return (row, lax.rem(y + d, NY) * 2 + core)

    def at_col(d):
        return (row, lax.rem(col + d, 8))

    up, down = at_z(1), at_z(NZ - 1)
    y_up, y_down = at_y(1), at_y(NY - 1)
    sibling = (row, y * 2 + 1 - core)

    def tile_start(xx):
        late = jnp.maximum(xx - 2, 0)
        return jnp.where(core == 0, 7 * xx - late, 6 * xx + late)

    def tile_count(xx):
        return jnp.where((xx < 2) == (core == 0), 7, 6)

    def window_start(xx):
        return jnp.minimum(tile_start(xx), NT - NCH)

    def x_of(d):
        return lax.rem(x + d, NX)

    def zrel(d):
        return lax.rem(z + d, NZ)

    start, count = tile_start(x), tile_count(x)

    def send(src, dst, ssem, rsem, target):
        pltpu.make_async_remote_copy(
            src_ref=src, dst_ref=dst, send_sem=ssem, recv_sem=rsem, device_id=target, device_id_type=MESH
        ).start()

    def wait(ref, sem):
        pltpu.make_async_copy(ref, ref, sem).wait()

    def tile(t, n=1):
        return pl.ds(pl.multiple_of(t * 128, 128), n * 128)

    def zblock(zz, begin=0, size=256):
        return pl.ds(pl.multiple_of(zz * 256 + begin, 64), size)

    barrier = pltpu.get_barrier_semaphore()
    partners = [at_z(d) for d in range(1, NZ)] + [at_x(d) for d in range(1, NX)] + [at_col(d) for d in range(1, 8)]
    for partner in partners:
        pl.semaphore_signal(barrier, inc=1, device_id=partner, device_id_type=MESH)

    loads = [(og, ogv), (act, avm), (pj, pv), (m1, m1v), (m2, m2v), (w, wv)]
    for k, (src, dst) in enumerate(loads):
        pltpu.make_async_copy(src, dst, loc.at[k]).start()

    def loaded(k):
        pltpu.make_async_copy(*loads[k], loc.at[k]).wait()

    own_lanes = pl.ds(pl.multiple_of(col * 256, 256), 256)

    def panel_rows(xx, begin=0, size=512):
        return pl.ds(pl.multiple_of(xx * 512 + begin, 256), size)

    def first_tile(u):
        return max(2 * u - 1, 0)

    def with_width(u, tiles, f):
        if u < NU - 1:
            f(1 if u == 0 else 2)
        else:
            pl.when(tiles == NCH)(lambda: f(2))
            pl.when(tiles == NCH - 1)(lambda: f(1))

    def low(n):
        return pl.ds(0, 128 * n)

    loaded(1)
    at[panel_rows(x), own_lanes] = avm[...].T
    loaded(0)
    g_rows = zblock(z, 64 * x, 64)
    for u in range(NU):

        def keep(n, u=u):
            g[u, g_rows, low(n)] = ogv[:, tile(start + first_tile(u), n)]
            if n == 1:
                g[u, :, pl.ds(128, 128)] = jnp.zeros((2048, 128), BF)

        with_width(u, count, keep)
    mw[:, :, :, pl.ds(NCH * 128, 128)] = jnp.zeros((4, 2, 8, 128), F32)
    pl.semaphore_wait(barrier, len(partners))

    def x_send(u):
        for d in (2, 1, 3):
            xx = x_of(d)

            def go(n, d=d, xx=xx):
                mine = ogv.at[:, tile(tile_start(xx) + first_tile(u), n)]
                send(mine, g.at[u, g_rows, low(n)], snd_x.at[d - 1, u], r_x.at[u], at_x(d))

            with_width(u, tile_count(xx), go)

    def z_hop(hop, u):
        lower, upper = zrel(NZ - hop), zrel(hop)

        def go(n):
            def move(zz, a, b, sem, target):
                part = g.at[u, zblock(zz, a, b), low(n)]
                send(part, part, snd_z.at[u], r_z.at[u, sem], target)

            def arrive(zz, sem):
                wait(g.at[u, zblock(zz), low(n)], r_z.at[u, sem])

            if hop == 0:
                wait(g.at[u, pl.ds(0, 192), low(n)], r_x.at[u])
                move(z, 0, 256, 0, up)
                move(z, 0, 256, 1, down)
            elif hop == 4:
                arrive(lower, 6)
            else:
                last = hop == 3
                arrive(lower, 2 * hop - 2)
                move(lower, 0, 128 if last else 256, 6 if last else 2 * hop, up)
                arrive(upper, 2 * hop - 1)
                move(upper, 128 if last else 0, 128 if last else 256, 6 if last else 2 * hop + 1, down)

        with_width(u, count, go)

    def a_ref(d, yy, begin, size):
        lanes = pl.ds(pl.multiple_of((yy * 2 + core) * 256, 256), 256)
        return at.at[panel_rows(x_of(d), begin, size), lanes]

    def a_send(d, yy, begin, size, sem, target):
        part = a_ref(d, yy, begin, size)
        send(part, part, snd_a.at[d], r_a.at[d, sem], target)

    def a_over_x(d, h):
        part = at.at[panel_rows(x, 256 * h, 256), own_lanes]
        send(part, part, snd_ax, r_ax.at[NX - d, h], at_x(d))

    over_x_seen = set()

    def over_x(d, h):
        if (d, h) not in over_x_seen:
            over_x_seen.add((d, h))
            wait(a_ref(d, y, 256 * h, 256), r_ax.at[d, h])

    def a_relay(d):
        h = 0 if d == 3 else 1
        over_x(d, h)
        part = a_ref(d, y, 256 * h, 256)
        send(part, part, snd_ax, r_ax.at[2, h], at_x(NX - d))

    def a_start(d, h):
        if d:
            over_x(d, h)
        a_send(d, y, 256 * h, 256, h, y_up)
        a_send(d, y, 256 * h, 256, 2 + h, y_down)
        a_send(d, y, 256 * h, 256, 6, sibling)

    y_lower, y_upper, y_far = lax.rem(y + 3, NY), lax.rem(y + 1, NY), lax.rem(y + 2, NY)

    def a_arrive(d, h):
        wait(a_ref(d, y_lower, 256 * h, 256), r_a.at[d, h])
        if h == 0:
            a_send(d, y_lower, 0, 256, 4, y_up)
        wait(a_ref(d, y_upper, 256 * h, 256), r_a.at[d, 2 + h])
        if h == 1:
            a_send(d, y_upper, 256, 256, 5, y_down)
        a_send(d, y_lower, 256 * h, 256, 6, sibling)
        a_send(d, y_upper, 256 * h, 256, 6, sibling)

    def a_far(d):
        wait(a_ref(d, y_far, 0, 256), r_a.at[d, 4])
        wait(a_ref(d, y_far, 256, 256), r_a.at[d, 5])
        a_send(d, y_far, 0, 512, 6, sibling)

    def a_done(d):
        wait(at.at[pl.ds(0, 512), pl.ds(0, 1024)], r_a.at[d, 6])

    def q_part():
        loaded(2)
        q = lax.dot_general(pv[...], avm[...], (((1,), (1,)), ((), ())), preferred_element_type=F32)
        for zz in range(NZ):
            qpart[zz] = q[32 * zz : 32 * zz + 32]
        for d in range(1, NZ):
            send(qpart.at[zrel(d)], qz.at[d - 1], snd_q.at[0], r_q.at[0], at_z(d))

    def q_over_z():
        wait(qz, r_q.at[0])
        q = qpart[z]
        for d in range(NZ - 1):
            q = q + qz[d]
        qs[...] = q
        for d in (2, 1, 3):
            send(qs, qx.at[d - 1], snd_q.at[1], r_q.at[1], at_x(d))

    def q_over_x():
        wait(qx, r_q.at[1])
        q = qs[...] + qx[0] + qx[1] + qx[2]
        high = q.astype(BF).astype(F32)
        rest = q - high
        parts = []
        for xx in range(NX):
            parts += [high[8 * xx : 8 * xx + 8], rest[8 * xx : 8 * xx + 8]]
        qa[:, own_lanes] = jnp.concatenate(parts, axis=0).astype(BF)
        part = qa.at[:, own_lanes]
        for d in range(1, 8):
            send(part, part, snd_q.at[2], r_q.at[2], at_col(d))

    def q_done():
        wait(qa.at[:, pl.ds(0, 1792)], r_q.at[2])

    def m_send():
        loaded(3)
        loaded(4)
        own = tile(window_start(x), NCH)
        mw[x, 0, :, low(NCH)] = m1v[:, own]
        mw[x, 1, :, low(NCH)] = m2v[:, own]
        for d in range(1, NX):
            cols = tile(window_start(x_of(d)), NCH)
            send(m1v.at[:, cols], mw.at[x, 0, :, low(NCH)], snd_m, r_m, at_x(d))
            send(m2v.at[:, cols], mw.at[x, 1, :, low(NCH)], snd_m, r_m, at_x(d))

    def m_done():
        wait(mw.at[pl.ds(0, 3), :, :, low(NCH)], r_m)

    def grad(d, u):
        total = jnp.dot(at[panel_rows(x_of(d)), :], g[u], preferred_element_type=F32).astype(BF)
        if d:
            gs[d - 1, u] = total

        def go(n):
            cols = tile(start + first_tile(u), n)
            if d:
                send(gs.at[d - 1, u, :, low(n)], gx.at[:, cols], snd_g.at[u], r_g.at[NX - d - 1, u], at_x(d))
            else:
                gx[:, cols] = total[:, : 128 * n]

        with_width(u, count, go)

    def sums(u):
        total = jnp.dot(qa[...], g[u], preferred_element_type=F32)
        lanes = tile(start - window_start(x) + first_tile(u), 2)
        normed_sq = jnp.zeros((8, 256), F32)
        proj_sq = jnp.zeros((8, 256), F32)
        wide = 1 if u == 0 else 2
        for xx in range(NX):
            proj = total[16 * xx : 16 * xx + 8] + total[16 * xx + 8 : 16 * xx + 16]
            pst[xx, :, tile(first_tile(u), wide)] = proj[:, : 128 * wide]
            first, second = moments(mw[xx, 0, :, lanes], mw[xx, 1, :, lanes], proj)
            normed = first / (1.0 - 0.9**STEP) / (jnp.sqrt(second / (1.0 - 0.999**STEP)) + 1e-08)
            normed_sq = normed_sq + normed * normed
            proj_sq = proj_sq + proj * proj
        normed_sq = jnp.sum(normed_sq, axis=0, keepdims=True)
        proj_sq = jnp.sum(proj_sq, axis=0, keepdims=True)
        s2s[u, 0:1] = normed_sq[:, :128]
        s2s[u, 1:2] = proj_sq[:, :128]
        s2s[u, 2:3] = normed_sq[:, 128:]
        s2s[u, 3:4] = proj_sq[:, 128:]
        s2s[u, 4:8] = jnp.zeros((4, 128), F32)
        for d in range(1, NZ):
            send(s2s.at[u], s2r.at[u, d - 1], snd_s2.at[u], r_s2.at[u], at_z(d))
        if u == NU - 1:
            for tiles in (NCH - 1, NCH):

                @pl.when(count == tiles)
                def _(tiles=tiles):
                    cols = tile(start, tiles)
                    prv[:, cols] = pst[x, :, low(tiles)]
                    for d in (2, 1, 3):
                        send(pst.at[x_of(d), :, low(tiles)], prv.at[:, cols], snd_pr, r_pr.at[NX - d - 1], at_x(d))

    def scale(u):
        wait(s2r.at[u], r_s2.at[u])
        total = s2s[u]
        for d in range(NZ - 1):
            total = total + s2r[u, d]
        left = jnp.sqrt(total[0:1]) / jnp.sqrt(total[1:2] + 1e-06)
        right = jnp.sqrt(total[2:3]) / jnp.sqrt(total[3:4] + 1e-06)
        scs[u] = jnp.broadcast_to(jnp.concatenate([left, right], axis=1), (8, 256))

        def go(n):
            cols = tile(start + first_tile(u), n)
            scr[:, cols] = scs[u, :, low(n)]
            for d in (2, 1, 3):
                send(scs.at[u, :, low(n)], scr.at[:, cols], snd_sc.at[u], r_sc.at[NX - d - 1, u], at_x(d))

        with_width(u, count, go)

    weights_seen = []

    def update(d, u):
        back = (NX - d) % NX
        xx = x_of(back)
        if not weights_seen:
            weights_seen.append(True)
            loaded(5)

        def go(n):
            cols = tile(tile_start(xx) + first_tile(u), n)
            if d:
                wait(scr.at[:, cols], r_sc.at[back - 1, u])
                wait(gx.at[:, cols], r_g.at[back - 1, u])
            step = 0.01 * scr[0:1, cols]
            wv[:, cols] = (wv[:, cols].astype(F32) - step * gx[:, cols].astype(F32)).astype(BF)
            pltpu.make_async_copy(wv.at[:, cols], ow.at[:, cols], outs.at[0]).start()

        with_width(u, tile_count(xx), go)

    def proj_out():
        for d in range(1, NX):
            xx = x_of(d)
            for tiles in (NCH - 1, NCH):

                @pl.when(tile_count(xx) == tiles)
                def _(tiles=tiles):
                    wait(prv.at[:, tile(tile_start(xx), tiles)], r_pr.at[d - 1])

        pltpu.make_async_copy(prv, o1, outs.at[1]).start()

    steps = dict(
        x_send=x_send, z_hop=z_hop, a_over_x=a_over_x, a_relay=a_relay, a_start=a_start, a_arrive=a_arrive,
        a_far=a_far, a_done=a_done, q_part=q_part, q_over_z=q_over_z, q_over_x=q_over_x, q_done=q_done,
        m_send=m_send, m_done=m_done, grad=grad, sums=sums, scale=scale, update=update, proj_out=proj_out,
    )
    for name, *numbers in ORDER:
        steps[name](*numbers)

    for u in range(NU):

        def drain(n, u=u):
            wait(g.at[u, pl.ds(0, 1792), low(n)], snd_z.at[u])
            wait(gs.at[:, u, :, low(n)], snd_g.at[u])
            wait(scr.at[:, low(3 * n)], snd_sc.at[u])

        with_width(u, count, drain)
        wait(s2r.at[u], snd_s2.at[u])
        for d in range(1, NX):
            with_width(u, tile_count(x_of(d)), lambda n, u=u, d=d: wait(ogv.at[:, low(n)], snd_x.at[d - 1, u]))
    for tiles in (NCH - 1, NCH):
        pl.when(count == tiles)(lambda tiles=tiles: wait(pst.at[pl.ds(0, 3), :, low(tiles)], snd_pr))
    for d in range(NX):
        wait(at.at[pl.ds(0, 512), pl.ds(0, 1792)], snd_a.at[d])
    wait(at.at[pl.ds(0, 512), pl.ds(0, 768)], snd_ax)
    wait(qz, snd_q.at[0])
    wait(qx, snd_q.at[1])
    wait(qa.at[:, pl.ds(0, 1792)], snd_q.at[2])
    wait(mw.at[pl.ds(0, 3), :, :, low(NCH)], snd_m)
    wait(prv, outs.at[1])
    wait(wv, outs.at[0])


def shards(activations, out_grads, weights, projector, first_moment, second_moment):
    vm, dma = pltpu.VMEM, pltpu.SemaphoreType.DMA
    operands = (activations, out_grads, weights, projector, first_moment, second_moment)
    operands = [pltpu.with_memory_space_constraint(operand, pltpu.HBM) for operand in operands]
    new_weights, proj = pl.pallas_call(
        kernel,
        out_shape=(
            jax.ShapeDtypeStruct((512, 3328), BF),
            jax.ShapeDtypeStruct((8, 3328), F32),
        ),
        in_specs=[pl.BlockSpec(memory_space=pl.ANY)] * 6,
        out_specs=(pl.BlockSpec(memory_space=pl.ANY),) * 2,
        scratch_shapes=[
            vm((256, 512), BF),
            vm((64, 3328), BF),
            vm((256, 512), BF),
            vm((512, 3328), BF),
            vm((8, 3328), F32),
            vm((8, 3328), F32),
            vm((2048, 2048), BF),
            vm((64, 2048), BF),
            vm((NU, 2048, 256), BF),
            vm((3, NU, 512, 256), BF),
            vm((512, 3328), BF),
            vm((8, 3328), F32),
            vm((4, 8, 1024), F32),
            vm((4, 2, 8, 1024), F32),
            vm((NU, 8, 128), F32),
            vm((NU, 7, 8, 128), F32),
            vm((NU, 8, 256), F32),
            vm((8, 3328), F32),
            vm((8, 32, 256), F32),
            vm((3, 32, 256), F32),
            vm((32, 256), F32),
            vm((7, 32, 256), F32),
            dma((6,)),
            dma((NU,)),
            dma((NU, 7)),
            dma((3, NU)),
            dma((3,)),
            dma((NU,)),
            dma((3, NU)),
            dma((NX, 7)),
            dma((NX, 2)),
            dma,
            dma((3,)),
            dma((3, NU)),
            dma((NU,)),
            dma((NU,)),
            dma,
            dma((NU,)),
            dma((NU,)),
            dma((NX,)),
            dma,
            dma,
            dma((3,)),
            dma((2,)),
        ],
        compiler_params=pltpu.CompilerParams(
            collective_id=0, has_side_effects=True, vmem_limit_bytes=48 * 1024 * 1024
        ),
    )(*operands)
    return (new_weights, *moments(first_moment, second_moment, proj))


def solution(mesh):
    return jax.shard_map(
        shards,
        mesh=mesh,
        in_specs=(
            P("col", "row"),
            P("row", "col"),
            P("row", "col"),
            P(None, "row"),
            P("row", "col"),
            P("row", "col"),
        ),
        out_specs=(P("row", "col"), P("row", "col"), P("row", "col")),
        check_vma=False,
    )
```

```python
import jax
import jax.numpy as jnp
from jax import lax
from jax.experimental import pallas as pl
from jax.experimental.pallas import tpu as pltpu
from jax.sharding import PartitionSpec as P

STEP = 10
MESH = pl.DeviceIdType.MESH
BF = jnp.bfloat16
F32 = jnp.float32

NZ, NX, NY = 8, 4, 4
NT = 26
NCH = 7
NU = 4

ORDER = [
    ("a_over_x", 3, 1), ("q_part",), ("x_send", 2), ("a_over_x", 1, 0), ("x_send", 1), ("a_start", 1, 1),
    ("a_over_x", 3, 0), ("z_hop", 0, 2), ("x_send", 0), ("a_start", 3, 0), ("a_over_x", 1, 1), ("z_hop", 0, 1),
    ("a_relay", 3), ("a_start", 1, 0), ("z_hop", 1, 2), ("a_start", 3, 1), ("z_hop", 1, 1), ("a_relay", 1),
    ("a_arrive", 3, 0), ("q_over_z",), ("a_arrive", 1, 1), ("a_arrive", 1, 0), ("z_hop", 2, 2), ("x_send", 3),
    ("a_arrive", 3, 1), ("a_start", 2, 0), ("z_hop", 2, 1), ("z_hop", 3, 2), ("m_send",), ("z_hop", 0, 0),
    ("a_far", 1), ("a_start", 2, 1), ("a_far", 3), ("z_hop", 3, 1), ("z_hop", 0, 3), ("a_done", 3), ("q_over_x",),
    ("a_done", 1), ("z_hop", 4, 2), ("grad", 1, 2), ("grad", 3, 2), ("a_arrive", 2, 0), ("z_hop", 1, 0),
    ("a_arrive", 2, 1), ("a_start", 0, 0), ("z_hop", 4, 1), ("m_done",), ("grad", 3, 1), ("z_hop", 1, 3),
    ("grad", 1, 1), ("q_done",), ("z_hop", 2, 0), ("a_start", 0, 1), ("sums", 1), ("a_far", 2), ("sums", 2),
    ("z_hop", 2, 3), ("a_done", 2), ("grad", 2, 2), ("z_hop", 3, 0), ("a_arrive", 0, 1), ("z_hop", 3, 3),
    ("z_hop", 4, 0), ("scale", 2), ("grad", 2, 0), ("scale", 1), ("sums", 0), ("a_arrive", 0, 0), ("z_hop", 4, 3),
    ("sums", 3), ("grad", 2, 3), ("grad", 3, 3), ("grad", 1, 3), ("update", 1, 2), ("a_far", 0), ("scale", 0),
    ("grad", 1, 0), ("update", 3, 1), ("a_done", 0), ("scale", 3), ("grad", 0, 1), ("proj_out",), ("grad", 0, 2),
    ("grad", 2, 1), ("grad", 0, 0), ("grad", 0, 3), ("update", 0, 2), ("grad", 3, 0), ("update", 1, 3),
    ("update", 1, 0), ("update", 2, 3), ("update", 0, 3), ("update", 1, 1), ("update", 3, 3), ("update", 3, 2),
    ("update", 0, 0), ("update", 0, 1), ("update", 2, 2), ("update", 2, 0), ("update", 2, 1), ("update", 3, 0),
]


def moments(first_moment, second_moment, proj):
    first = 0.9 * first_moment + 0.1 * proj
    second = 0.999 * second_moment + 0.001 * proj * proj
    return first, second


def kernel(
    act, og, w, pj, m1, m2, ow, o1,
    avm, ogv, pv, wv, m1v, m2v, at, qa, g, gs, gx, prv, pst, mw, s2s, s2r, scs, scr, qpart, qx, qs, qz,
    loc, r_x, r_z, r_g, r_pr, r_s2, r_sc, r_a, r_ax, r_m, r_q,
    snd_x, snd_z, snd_g, snd_pr, snd_s2, snd_sc, snd_a, snd_ax, snd_m, snd_q, outs,
):
    row, col = lax.axis_index("row"), lax.axis_index("col")
    z, x = row // 4, lax.rem(row, 4)
    y, core = col // 2, lax.rem(col, 2)

    def at_z(d):
        return (lax.rem(z + d, NZ) * 4 + x, col)

    def at_x(d):
        return (z * 4 + lax.rem(x + d, NX), col)

    def at_y(d):
        return (row, lax.rem(y + d, NY) * 2 + core)

    def at_col(d):
        return (row, lax.rem(col + d, 8))

    up, down = at_z(1), at_z(NZ - 1)
    y_up, y_down = at_y(1), at_y(NY - 1)
    sibling = (row, y * 2 + 1 - core)

    def tile_start(xx):
        late = jnp.maximum(xx - 2, 0)
        return jnp.where(core == 0, 7 * xx - late, 6 * xx + late)

    def tile_count(xx):
        return jnp.where((xx < 2) == (core == 0), 7, 6)

    def window_start(xx):
        return jnp.minimum(tile_start(xx), NT - NCH)

    def x_of(d):
        return lax.rem(x + d, NX)

    def zrel(d):
        return lax.rem(z + d, NZ)

    start, count = tile_start(x), tile_count(x)

    def send(src, dst, ssem, rsem, target):
        pltpu.make_async_remote_copy(
            src_ref=src, dst_ref=dst, send_sem=ssem, recv_sem=rsem, device_id=target, device_id_type=MESH
        ).start()

    def wait(ref, sem):
        pltpu.make_async_copy(ref, ref, sem).wait()

    def tile(t, n=1):
        return pl.ds(pl.multiple_of(t * 128, 128), n * 128)

    def zblock(zz, begin=0, size=256):
        return pl.ds(pl.multiple_of(zz * 256 + begin, 64), size)

    barrier = pltpu.get_barrier_semaphore()
    partners = [at_z(d) for d in range(1, NZ)] + [at_x(d) for d in range(1, NX)] + [at_col(d) for d in range(1, 8)]
    for partner in partners:
        pl.semaphore_signal(barrier, inc=1, device_id=partner, device_id_type=MESH)

    loads = [(og, ogv), (act, avm), (pj, pv), (m1, m1v), (m2, m2v), (w, wv)]
    for k, (src, dst) in enumerate(loads):
        pltpu.make_async_copy(src, dst, loc.at[k]).start()

    def loaded(k):
        pltpu.make_async_copy(*loads[k], loc.at[k]).wait()

    own_lanes = pl.ds(pl.multiple_of(col * 256, 256), 256)

    def panel_rows(xx, begin=0, size=512):
        return pl.ds(pl.multiple_of(xx * 512 + begin, 256), size)

    def first_tile(u):
        return max(2 * u - 1, 0)

    def with_width(u, tiles, f):
        if u < NU - 1:
            f(1 if u == 0 else 2)
        else:
            pl.when(tiles == NCH)(lambda: f(2))
            pl.when(tiles == NCH - 1)(lambda: f(1))

    def low(n):
        return pl.ds(0, 128 * n)

    loaded(1)
    at[panel_rows(x), own_lanes] = avm[...].T
    loaded(0)
    g_rows = zblock(z, 64 * x, 64)
    for u in range(NU):

        def keep(n, u=u):
            g[u, g_rows, low(n)] = ogv[:, tile(start + first_tile(u), n)]
            if n == 1:
                g[u, :, pl.ds(128, 128)] = jnp.zeros((2048, 128), BF)

        with_width(u, count, keep)
    mw[:, :, :, pl.ds(NCH * 128, 128)] = jnp.zeros((4, 2, 8, 128), F32)
    pl.semaphore_wait(barrier, len(partners))

    def x_send(u):
        for d in (2, 1, 3):
            xx = x_of(d)

            def go(n, d=d, xx=xx):
                mine = ogv.at[:, tile(tile_start(xx) + first_tile(u), n)]
                send(mine, g.at[u, g_rows, low(n)], snd_x.at[d - 1, u], r_x.at[u], at_x(d))

            with_width(u, tile_count(xx), go)

    def z_hop(hop, u):
        lower, upper = zrel(NZ - hop), zrel(hop)

        def go(n):
            def move(zz, a, b, sem, target):
                part = g.at[u, zblock(zz, a, b), low(n)]
                send(part, part, snd_z.at[u], r_z.at[u, sem], target)

            def arrive(zz, sem):
                wait(g.at[u, zblock(zz), low(n)], r_z.at[u, sem])

            if hop == 0:
                wait(g.at[u, pl.ds(0, 192), low(n)], r_x.at[u])
                move(z, 0, 256, 0, up)
                move(z, 0, 256, 1, down)
            elif hop == 4:
                arrive(lower, 6)
            else:
                last = hop == 3
                arrive(lower, 2 * hop - 2)
                move(lower, 0, 128 if last else 256, 6 if last else 2 * hop, up)
                arrive(upper, 2 * hop - 1)
                move(upper, 128 if last else 0, 128 if last else 256, 6 if last else 2 * hop + 1, down)

        with_width(u, count, go)

    def a_ref(d, yy, begin, size):
        lanes = pl.ds(pl.multiple_of((yy * 2 + core) * 256, 256), 256)
        return at.at[panel_rows(x_of(d), begin, size), lanes]

    def a_send(d, yy, begin, size, sem, target):
        part = a_ref(d, yy, begin, size)
        send(part, part, snd_a.at[d], r_a.at[d, sem], target)

    def a_over_x(d, h):
        part = at.at[panel_rows(x, 256 * h, 256), own_lanes]
        send(part, part, snd_ax, r_ax.at[NX - d, h], at_x(d))

    over_x_seen = set()

    def over_x(d, h):
        if (d, h) not in over_x_seen:
            over_x_seen.add((d, h))
            wait(a_ref(d, y, 256 * h, 256), r_ax.at[d, h])

    def a_relay(d):
        h = 0 if d == 3 else 1
        over_x(d, h)
        part = a_ref(d, y, 256 * h, 256)
        send(part, part, snd_ax, r_ax.at[2, h], at_x(NX - d))

    def a_start(d, h):
        if d:
            over_x(d, h)
        a_send(d, y, 256 * h, 256, h, y_up)
        a_send(d, y, 256 * h, 256, 2 + h, y_down)
        a_send(d, y, 256 * h, 256, 6, sibling)

    y_lower, y_upper, y_far = lax.rem(y + 3, NY), lax.rem(y + 1, NY), lax.rem(y + 2, NY)

    def a_arrive(d, h):
        wait(a_ref(d, y_lower, 256 * h, 256), r_a.at[d, h])
        if h == 0:
            a_send(d, y_lower, 0, 256, 4, y_up)
        wait(a_ref(d, y_upper, 256 * h, 256), r_a.at[d, 2 + h])
        if h == 1:
            a_send(d, y_upper, 256, 256, 5, y_down)
        a_send(d, y_lower, 256 * h, 256, 6, sibling)
        a_send(d, y_upper, 256 * h, 256, 6, sibling)

    def a_far(d):
        wait(a_ref(d, y_far, 0, 256), r_a.at[d, 4])
        wait(a_ref(d, y_far, 256, 256), r_a.at[d, 5])
        a_send(d, y_far, 0, 512, 6, sibling)

    def a_done(d):
        wait(at.at[pl.ds(0, 512), pl.ds(0, 1024)], r_a.at[d, 6])

    def q_part():
        loaded(2)
        q = lax.dot_general(pv[...], avm[...], (((1,), (1,)), ((), ())), preferred_element_type=F32)
        for zz in range(NZ):
            qpart[zz] = q[32 * zz : 32 * zz + 32]
        for d in range(1, NZ):
            send(qpart.at[zrel(d)], qz.at[d - 1], snd_q.at[0], r_q.at[0], at_z(d))

    def q_over_z():
        wait(qz, r_q.at[0])
        q = qpart[z]
        for d in range(NZ - 1):
            q = q + qz[d]
        qs[...] = q
        for d in (2, 1, 3):
            send(qs, qx.at[d - 1], snd_q.at[1], r_q.at[1], at_x(d))

    def q_over_x():
        wait(qx, r_q.at[1])
        q = qs[...] + qx[0] + qx[1] + qx[2]
        high = q.astype(BF).astype(F32)
        rest = q - high
        parts = []
        for xx in range(NX):
            parts += [high[8 * xx : 8 * xx + 8], rest[8 * xx : 8 * xx + 8]]
        qa[:, own_lanes] = jnp.concatenate(parts, axis=0).astype(BF)
        part = qa.at[:, own_lanes]
        for d in range(1, 8):
            send(part, part, snd_q.at[2], r_q.at[2], at_col(d))

    def q_done():
        wait(qa.at[:, pl.ds(0, 1792)], r_q.at[2])

    def m_send():
        loaded(3)
        loaded(4)
        own = tile(window_start(x), NCH)
        mw[x, 0, :, low(NCH)] = m1v[:, own]
        mw[x, 1, :, low(NCH)] = m2v[:, own]
        for d in range(1, NX):
            cols = tile(window_start(x_of(d)), NCH)
            send(m1v.at[:, cols], mw.at[x, 0, :, low(NCH)], snd_m, r_m, at_x(d))
            send(m2v.at[:, cols], mw.at[x, 1, :, low(NCH)], snd_m, r_m, at_x(d))

    def m_done():
        wait(mw.at[pl.ds(0, 3), :, :, low(NCH)], r_m)

    def grad(d, u):
        total = jnp.dot(at[panel_rows(x_of(d)), :], g[u], preferred_element_type=F32).astype(BF)
        if d:
            gs[d - 1, u] = total

        def go(n):
            cols = tile(start + first_tile(u), n)
            if d:
                send(gs.at[d - 1, u, :, low(n)], gx.at[:, cols], snd_g.at[u], r_g.at[NX - d - 1, u], at_x(d))
            else:
                gx[:, cols] = total[:, : 128 * n]

        with_width(u, count, go)

    def sums(u):
        total = jnp.dot(qa[...], g[u], preferred_element_type=F32)
        lanes = tile(start - window_start(x) + first_tile(u), 2)
        normed_sq = jnp.zeros((8, 256), F32)
        proj_sq = jnp.zeros((8, 256), F32)
        wide = 1 if u == 0 else 2
        for xx in range(NX):
            proj = total[16 * xx : 16 * xx + 8] + total[16 * xx + 8 : 16 * xx + 16]
            pst[xx, :, tile(first_tile(u), wide)] = proj[:, : 128 * wide]
            first, second = moments(mw[xx, 0, :, lanes], mw[xx, 1, :, lanes], proj)
            normed = first / (1.0 - 0.9**STEP) / (jnp.sqrt(second / (1.0 - 0.999**STEP)) + 1e-08)
            normed_sq = normed_sq + normed * normed
            proj_sq = proj_sq + proj * proj
        normed_sq = jnp.sum(normed_sq, axis=0, keepdims=True)
        proj_sq = jnp.sum(proj_sq, axis=0, keepdims=True)
        s2s[u, 0:1] = normed_sq[:, :128]
        s2s[u, 1:2] = proj_sq[:, :128]
        s2s[u, 2:3] = normed_sq[:, 128:]
        s2s[u, 3:4] = proj_sq[:, 128:]
        s2s[u, 4:8] = jnp.zeros((4, 128), F32)
        for d in range(1, NZ):
            send(s2s.at[u], s2r.at[u, d - 1], snd_s2.at[u], r_s2.at[u], at_z(d))
        if u == NU - 1:
            for tiles in (NCH - 1, NCH):

                @pl.when(count == tiles)
                def _(tiles=tiles):
                    cols = tile(start, tiles)
                    prv[:, cols] = pst[x, :, low(tiles)]
                    for d in (2, 1, 3):
                        send(pst.at[x_of(d), :, low(tiles)], prv.at[:, cols], snd_pr, r_pr.at[NX - d - 1], at_x(d))

    def scale(u):
        wait(s2r.at[u], r_s2.at[u])
        total = s2s[u]
        for d in range(NZ - 1):
            total = total + s2r[u, d]
        left = jnp.sqrt(total[0:1]) / jnp.sqrt(total[1:2] + 1e-06)
        right = jnp.sqrt(total[2:3]) / jnp.sqrt(total[3:4] + 1e-06)
        scs[u] = jnp.broadcast_to(jnp.concatenate([left, right], axis=1), (8, 256))

        def go(n):
            cols = tile(start + first_tile(u), n)
            scr[:, cols] = scs[u, :, low(n)]
            for d in (2, 1, 3):
                send(scs.at[u, :, low(n)], scr.at[:, cols], snd_sc.at[u], r_sc.at[NX - d - 1, u], at_x(d))

        with_width(u, count, go)

    weights_seen = []

    def update(d, u):
        back = (NX - d) % NX
        xx = x_of(back)
        if not weights_seen:
            weights_seen.append(True)
            loaded(5)

        def go(n):
            cols = tile(tile_start(xx) + first_tile(u), n)
            if d:
                wait(scr.at[:, cols], r_sc.at[back - 1, u])
                wait(gx.at[:, cols], r_g.at[back - 1, u])
            step = 0.01 * scr[0:1, cols]
            wv[:, cols] = (wv[:, cols].astype(F32) - step * gx[:, cols].astype(F32)).astype(BF)
            pltpu.make_async_copy(wv.at[:, cols], ow.at[:, cols], outs.at[0]).start()

        with_width(u, tile_count(xx), go)

    def proj_out():
        for d in range(1, NX):
            xx = x_of(d)
            for tiles in (NCH - 1, NCH):

                @pl.when(tile_count(xx) == tiles)
                def _(tiles=tiles):
                    wait(prv.at[:, tile(tile_start(xx), tiles)], r_pr.at[d - 1])

        pltpu.make_async_copy(prv, o1, outs.at[1]).start()

    def sends_done():
        for u in range(NU):

            def drain(n, u=u):
                wait(g.at[u, pl.ds(0, 1792), low(n)], snd_z.at[u])
                wait(gs.at[:, u, :, low(n)], snd_g.at[u])
                wait(scr.at[:, low(3 * n)], snd_sc.at[u])

            with_width(u, count, drain)
            wait(s2r.at[u], snd_s2.at[u])
            for d in range(1, NX):
                with_width(u, tile_count(x_of(d)), lambda n, u=u, d=d: wait(ogv.at[:, low(n)], snd_x.at[d - 1, u]))
        for tiles in (NCH - 1, NCH):
            pl.when(count == tiles)(lambda tiles=tiles: wait(pst.at[pl.ds(0, 3), :, low(tiles)], snd_pr))
        for d in range(NX):
            wait(at.at[pl.ds(0, 512), pl.ds(0, 1792)], snd_a.at[d])
        wait(at.at[pl.ds(0, 512), pl.ds(0, 768)], snd_ax)
        wait(qz, snd_q.at[0])
        wait(qx, snd_q.at[1])
        wait(qa.at[:, pl.ds(0, 1792)], snd_q.at[2])
        wait(mw.at[pl.ds(0, 3), :, :, low(NCH)], snd_m)

    steps = dict(
        x_send=x_send, z_hop=z_hop, a_over_x=a_over_x, a_relay=a_relay, a_start=a_start, a_arrive=a_arrive,
        a_far=a_far, a_done=a_done, q_part=q_part, q_over_z=q_over_z, q_over_x=q_over_x, q_done=q_done,
        m_send=m_send, m_done=m_done, grad=grad, sums=sums, scale=scale, update=update, proj_out=proj_out,
    )
    for position, (name, *numbers) in enumerate(ORDER):
        if position == len(ORDER) - 2:
            sends_done()
        steps[name](*numbers)

    wait(prv, outs.at[1])
    wait(wv, outs.at[0])


def shards(activations, out_grads, weights, projector, first_moment, second_moment):
    vm, dma = pltpu.VMEM, pltpu.SemaphoreType.DMA
    operands = (activations, out_grads, weights, projector, first_moment, second_moment)
    operands = [pltpu.with_memory_space_constraint(operand, pltpu.HBM) for operand in operands]
    new_weights, proj = pl.pallas_call(
        kernel,
        out_shape=(
            jax.ShapeDtypeStruct((512, 3328), BF),
            jax.ShapeDtypeStruct((8, 3328), F32),
        ),
        in_specs=[pl.BlockSpec(memory_space=pl.ANY)] * 6,
        out_specs=(pl.BlockSpec(memory_space=pl.ANY),) * 2,
        scratch_shapes=[
            vm((256, 512), BF),
            vm((64, 3328), BF),
            vm((256, 512), BF),
            vm((512, 3328), BF),
            vm((8, 3328), F32),
            vm((8, 3328), F32),
            vm((2048, 2048), BF),
            vm((64, 2048), BF),
            vm((NU, 2048, 256), BF),
            vm((3, NU, 512, 256), BF),
            vm((512, 3328), BF),
            vm((8, 3328), F32),
            vm((4, 8, 1024), F32),
            vm((4, 2, 8, 1024), F32),
            vm((NU, 8, 128), F32),
            vm((NU, 7, 8, 128), F32),
            vm((NU, 8, 256), F32),
            vm((8, 3328), F32),
            vm((8, 32, 256), F32),
            vm((3, 32, 256), F32),
            vm((32, 256), F32),
            vm((7, 32, 256), F32),
            dma((6,)),
            dma((NU,)),
            dma((NU, 7)),
            dma((3, NU)),
            dma((3,)),
            dma((NU,)),
            dma((3, NU)),
            dma((NX, 7)),
            dma((NX, 2)),
            dma,
            dma((3,)),
            dma((3, NU)),
            dma((NU,)),
            dma((NU,)),
            dma,
            dma((NU,)),
            dma((NU,)),
            dma((NX,)),
            dma,
            dma,
            dma((3,)),
            dma((2,)),
        ],
        compiler_params=pltpu.CompilerParams(
            collective_id=0, has_side_effects=True, vmem_limit_bytes=48 * 1024 * 1024
        ),
    )(*operands)
    return (new_weights, *moments(first_moment, second_moment, proj))


def solution(mesh):
    return jax.shard_map(
        shards,
        mesh=mesh,
        in_specs=(
            P("col", "row"),
            P("row", "col"),
            P("row", "col"),
            P(None, "row"),
            P("row", "col"),
            P("row", "col"),
        ),
        out_specs=(P("row", "col"), P("row", "col"), P("row", "col")),
        check_vma=False,
    )
```
